512 devices in a mesh: emb: 128 (over y, z, core), col: 4 (over x).
Axes of the slice: x: 4, y: 4, z: 16, core: 2. Of those that a mesh axis runs over, the one named last changes fastest.
Arguments:
- user_table: bfloat16 [1024, 16384], P('emb', 'col'), may hold values from -4 to 4
- user_scale: bfloat16 [1024], P('emb'), may hold values from 0.5 to 2
- item_table: bfloat16 [4096, 1024], P('emb', 'col'), may hold values from -3 to 3
- user_owner: int32 [16384, 1], P('emb'), may hold values from 0 to 127; in each aligned block of 128 rows (0 to 127, 128 to 255, ...) at most 2 rows name the same one
- user_row: int32 [16384], P('emb'), may hold values from 0 to 7
- item_owner: int32 [16384, 4], P('emb'), may hold values from 0 to 127, all different within a row; in each aligned block of 128 rows (0 to 127, 128 to 255, ...) at most 8 rows name the same one
- item_row: int32 [16384, 4], P('emb'), may hold values from 0 to 31
- labels: float32 [16384], P('emb'), may hold values from 0 to 1
- enter_user: bfloat16 [16384, 128], P('col'), may hold values from -0.046875 to 0.046875
- enter_item: bfloat16 [1024, 128], P('col'), may hold values from -0.046875 to 0.046875
- leave_user: bfloat16 [128, 16384], P(None, 'col'), may hold values from -0.5 to 0.5
- leave_item: bfloat16 [128, 1024], P(None, 'col'), may hold values from -0.5 to 0.5
- bias_user: float32 [16384], P('col'), may hold values from -3 to 3
- bias_item: float32 [1024], P('col'), may hold values from -3 to 3
- head_user: float32 [16384], P('col'), may hold values from -0.046875 to 0.046875
- head_item: float32 [1024], P('col'), may hold values from -0.046875 to 0.046875
Outputs:
- user_grad: float32 [1024, 16384], P('emb', 'col')
- item_grad: float32 [4096, 1024], P('emb', 'col')
The draws below stay inside these ranges and needn't reach their ends.
Inputs may be any that keep to these rules, and one draw needn't show every extreme that they name: `user_owner`: among the impressions of one device no owner is named more than 2 times; in some devices one owner is named exactly 2 times. `item_owner`: the 4 owners of one impression differ. Among the item entries of one device no owner is named more than 8 times; in some devices one owner exactly 8 times.
All inputs are finite; a program needn't handle non-finite values.
Results may differ from the reference program's by a relative error of at most 0.035.
Values may be sent and summed in bfloat16 or wider, within the bound.
No kernel may reach another device: no remote copies, remote signals or barrier semaphores. Data moves between devices by JAX's collectives and lax.ppermute only.
A program may use at most 64 MiB of HBM per device.

```python
import math
import jax
import jax.numpy as jnp
import numpy as np
from jax import lax

RANK = 128
LIST = 4
IMP_DEV = 128
DU = 16384
DI = 1024
OWNERS = 128
CAP_U = 2
CAP_I = 8
USERS_DEV = 8
ITEMS_DEV = 32
IMPRESSIONS = 16384
USERS = 1024
ITEMS = 4096
N_EMB = 128


def place_ends(drawn, stream_key, low, largest):
    longest = drawn.shape.index(max(drawn.shape))
    spots = []
    for shift in (0, 1):
        where = [jax.random.randint(jax.random.fold_in(stream_key, axis), (), 0, length) for axis, length in enumerate(drawn.shape)]
        where[longest] = (where[longest] + shift) % drawn.shape[longest]
        spots.append(tuple(where))
    return drawn.at[spots[0]].set(low).at[spots[1]].set(largest)


def block_scale(stream_key, extent, cuts, smallest, largest):
    gain = 1.0
    for axis_at, parts in cuts:
        steps = jax.random.uniform(jax.random.fold_in(jax.random.fold_in(stream_key, 6), axis_at), (parts,), jnp.float32, smallest / len(cuts), largest / len(cuts))
        gain = gain * jnp.repeat(jnp.exp(steps), extent[axis_at] // parts).reshape((-1,) + (1,) * (len(extent) - 1 - axis_at))
    return gain


def deal_out(key, own, number, rows, amount, top, bound, slope):
    ranking = jax.random.permutation(key, amount)
    heavy_load, common = shares(amount, rows * top, bound, slope, True), shares(amount, rows * top, bound, slope, False)
    places = jnp.arange(amount)

    def named(sizes, offset_by):
        used = int((sizes > 0).sum())
        fixed = max(1, used // 4)
        passed = fixed + (places - fixed + offset_by * (used - fixed)) % max(1, amount - fixed)
        return jnp.zeros((amount,), jnp.int32).at[ranking[jnp.where(places < fixed, places, passed)]].set(jnp.asarray(sizes, jnp.int32))

    sizes = jnp.where(number % 4 == 0, named(heavy_load, number // 4), named(common, number - number // 4 - 1))
    mixed = jax.random.permutation(jax.random.fold_in(own, 3), amount)
    source_of, receiver = mixed[0:amount // 2 * 2:2], mixed[1:amount // 2 * 2:2]
    margin = jnp.minimum(sizes[source_of] - 1, bound - sizes[receiver]) // 2
    margin = jnp.where((source_of == ranking[0]) | (receiver == ranking[0]) | (sizes[receiver] == 0), 0, jnp.maximum(margin, 0))
    passed = jax.random.randint(jax.random.fold_in(own, 4), (amount // 2,), 0, 1 << 20) % (margin + 1)
    sizes = sizes.at[source_of].add(-passed).at[receiver].add(passed)
    items = jnp.searchsorted(jnp.cumsum(sizes), jnp.arange(rows * top), side="right").astype(jnp.int32)
    table = items.reshape(top, rows).T
    table = table[jax.random.permutation(jax.random.fold_in(own, 1), rows)]
    offset_by = jax.random.randint(jax.random.fold_in(own, 2), (rows, 1), 0, top)
    return jnp.take_along_axis(table, (jnp.arange(top)[None, :] + offset_by) % top, axis=1)


def shares(amount, total, reach, skew, full):
    portions = [(1 << 20) // math.isqrt(grade ** skew) + 1 for grade in range(1, amount + 1)]
    largest = reach if full else min(reach, max(-(-total // amount), total * portions[0] // sum(portions)))
    least = 1 if total - largest >= amount - 1 else 0
    counts, surplus = [largest] + [least] * (amount - 1), total - largest - least * (amount - 1)
    while surplus > 0:
        movable = [i for i in range(1, amount) if counts[i] < largest] or [i for i in range(1, amount) if counts[i] < reach]
        mass, left = sum([portions[i] for i in movable]), surplus
        for i in movable:
            more = min(reach - counts[i], max(1, left * portions[i] // mass), surplus)
            counts[i] = counts[i] + more
            surplus = surplus - more
    return np.array(counts)


def gaussian(key, dims, spread, bound, split=(), kind=jnp.bfloat16):
    result = jax.random.normal(key, dims, jnp.float32) * spread
    if len(split) > 0:
        result = block_scale(key, dims, split, -0.22, 0.18) * result
    return jnp.clip(result, min=-bound, max=bound).astype(kind)


def setup_inputs(seed: int = 0) -> dict:
    seeds = jax.random.split(jax.random.key(seed), 17)
    user_table = gaussian(seeds[0], (USERS, DU), 1.0, 4.0, ((0, 128), (1, 4)))
    user_scale = jnp.clip(jnp.exp(math.log(2.0) - 1.3862944 * jax.random.uniform(seeds[1], (USERS,), jnp.float32) ** block_scale(seeds[1], (USERS,), ((0, 128),), -0.2, 0.2)), 0.5, 2.0).astype(jnp.bfloat16)
    item_table = gaussian(seeds[2], (ITEMS, DI), 0.5, 3.0, ((0, 128), (1, 4)))
    user_owner_keys = jax.random.split(jax.random.fold_in(seeds[3], 1), IMPRESSIONS // IMP_DEV)
    user_owner_turns = jax.random.permutation(jax.random.fold_in(seeds[3], 3), IMPRESSIONS // IMP_DEV)
    user_owner = jax.vmap(lambda own, number: deal_out(jax.random.fold_in(seeds[3], 2), own, number, IMP_DEV, OWNERS, 1, CAP_U, 2))(user_owner_keys, user_owner_turns).reshape((IMPRESSIONS, 1))
    user_row = place_ends(jax.random.randint(seeds[4], (IMPRESSIONS,), 0, USERS_DEV), jax.random.fold_in(seeds[4], 1), 0, USERS_DEV - 1).astype(jnp.int32)
    item_owner_keys = jax.random.split(jax.random.fold_in(seeds[5], 1), IMPRESSIONS // IMP_DEV)
    item_owner_turns = jax.random.permutation(jax.random.fold_in(seeds[5], 3), IMPRESSIONS // IMP_DEV)
    item_owner = jax.vmap(lambda own, number: deal_out(jax.random.fold_in(seeds[5], 2), own, number, IMP_DEV, OWNERS, LIST, CAP_I, 2))(item_owner_keys, item_owner_turns).reshape((IMPRESSIONS, LIST))
    item_row = place_ends(jax.random.randint(seeds[6], (IMPRESSIONS, LIST), 0, ITEMS_DEV), jax.random.fold_in(seeds[6], 1), 0, ITEMS_DEV - 1).astype(jnp.int32)
    labels = jnp.clip(1.0 * jax.random.uniform(seeds[7], (IMPRESSIONS,), jnp.float32) ** block_scale(seeds[7], (IMPRESSIONS,), ((0, 128),), -0.2, 0.2), 0.0, 1.0)
    enter_user = gaussian(seeds[8], (DU, RANK), (DU + DI) ** -0.5, 0.046875, ((0, 4),))
    enter_item = gaussian(seeds[9], (DI, RANK), (DU + DI) ** -0.5, 0.046875, ((0, 4),))
    leave_user = gaussian(seeds[10], (RANK, DU), RANK ** -0.5, 0.5, ((1, 4),))
    leave_item = gaussian(seeds[11], (RANK, DI), RANK ** -0.5, 0.5, ((1, 4),))
    bias_user = gaussian(seeds[12], (DU,), 0.5, 3.0, ((0, 4),), jnp.float32)
    bias_item = gaussian(seeds[13], (DI,), 0.5, 3.0, ((0, 4),), jnp.float32)
    head_user = gaussian(seeds[14], (DU,), (DU + DI) ** -0.5, 0.046875, ((0, 4),), jnp.float32)
    head_item = gaussian(seeds[15], (DI,), (DU + DI) ** -0.5, 0.046875, ((0, 4),), jnp.float32)
    return dict(user_table=user_table, user_scale=user_scale, item_table=item_table, user_owner=user_owner, user_row=user_row, item_owner=item_owner, item_row=item_row, labels=labels, enter_user=enter_user, enter_item=enter_item, leave_user=leave_user, leave_item=leave_item, bias_user=bias_user, bias_item=bias_item, head_user=head_user, head_item=head_item)


loss_scale = 128.0


def reference(user_table, user_scale, item_table, user_owner, user_row, item_owner, item_row, labels, enter_user, enter_item, leave_user, leave_item, bias_user, bias_item, head_user, head_item):
    user_ids = (user_owner[:, 0] * USERS_DEV + user_row).astype(jnp.int32)
    item_ids = (item_owner * ITEMS_DEV + item_row).astype(jnp.int32)
    inputs = (user_ids.reshape(N_EMB, IMP_DEV), item_ids.reshape(N_EMB, IMP_DEV, LIST), labels.reshape(N_EMB, IMP_DEV))

    def one_block(totals, pieces):
        user_total, item_total = totals
        block_users, block_items, targets = pieces
        user_input = (user_table[block_users].astype(jnp.float32) * user_scale[block_users].astype(jnp.float32)[:, None]).astype(jnp.bfloat16)
        pooled = jnp.sum(item_table[block_items].astype(jnp.float32), axis=1).astype(jnp.bfloat16)
        lowrank = (jnp.dot(user_input, enter_user, preferred_element_type=jnp.float32) + jnp.dot(pooled, enter_item, preferred_element_type=jnp.float32)).astype(jnp.bfloat16)
        hidden_user = jnp.dot(lowrank, leave_user, preferred_element_type=jnp.float32)
        hidden_item = jnp.dot(lowrank, leave_item, preferred_element_type=jnp.float32)
        user_float = user_input.astype(jnp.float32)
        item_float = pooled.astype(jnp.float32)
        logits = jnp.sum(head_user * (user_float * (hidden_user + bias_user) + user_float), axis=1) + jnp.sum(head_item * (item_float * (hidden_item + bias_item) + item_float), axis=1)
        user_scaled = (user_float * head_user).astype(jnp.bfloat16)
        item_scaled = (item_float * head_item).astype(jnp.bfloat16)
        carried = jnp.dot(user_scaled, leave_user.T, preferred_element_type=jnp.float32) + jnp.dot(item_scaled, leave_item.T, preferred_element_type=jnp.float32)
        logit_grad = loss_scale * (jax.nn.sigmoid(logits) - targets)
        back_rank = (logit_grad[:, None] * carried).astype(jnp.bfloat16)
        user_delta = (logit_grad[:, None] * head_user * (hidden_user + bias_user + 1.0) + jnp.dot(back_rank, enter_user.T, preferred_element_type=jnp.float32)).astype(jnp.bfloat16)
        item_delta = (logit_grad[:, None] * head_item * (hidden_item + bias_item + 1.0) + jnp.dot(back_rank, enter_item.T, preferred_element_type=jnp.float32)).astype(jnp.bfloat16)
        user_delta = lax.optimization_barrier(user_delta)
        item_delta = lax.optimization_barrier(item_delta)
        user_total = user_total.at[block_users].add(user_delta.astype(jnp.float32))
        item_total = item_total.at[block_items.reshape(-1)].add(jnp.repeat(item_delta, LIST, axis=0).astype(jnp.float32))
        return (user_total, item_total), None

    start = (jnp.zeros((USERS, DU), jnp.float32), jnp.zeros((ITEMS, DI), jnp.float32))
    finals, unused = lax.scan(one_block, start, inputs)
    return finals[0], finals[1]
```

```python
import jax
import jax.numpy as jnp
from jax import lax
from jax.experimental import pallas as pl
from jax.experimental.pallas import tpu as pltpu
from jax.sharding import Mesh, PartitionSpec as P

loss_scale = 128.0
bf16 = jnp.bfloat16
f32 = jnp.float32
i32 = jnp.int32
EMB = ("y", "z", "c")
BLOCK = ("y", "c", "x")
LANES = 128
FRONT = 24


def dot(a, b, ca=1, cb=0):
    return lax.dot_general(a, b, (((ca,), (cb,)), ((), ())), preferred_element_type=f32)


def iota(shape, axis):
    return lax.broadcasted_iota(i32, shape, axis)


def roll(value, shift):
    shift = shift % LANES
    return pltpu.roll(value, shift, 1) if shift else value


def column(row, rows, first):
    hit = iota((rows, LANES), 1) == iota((rows, LANES), 0) + first
    return jnp.sum(jnp.where(hit, row, 0.0), axis=1, keepdims=True)


def pack(full, extra):
    held = full.shape[0]
    lane = iota((held, LANES), 1)
    line = jnp.sum(jnp.where(lane == iota((held, LANES), 0) + 64, extra, 0.0), axis=0, keepdims=True)
    tail = jnp.where(iota((2 * FRONT - held, LANES), 0) == 0, line, 0.0)
    right = jnp.concatenate([roll(full[FRONT:], 64), tail], axis=0)
    return jnp.where(lane[:FRONT] < 64, full[:FRONT], right)


def unpack(block, held):
    lane = iota((held, LANES), 1)
    full = jnp.concatenate([block, roll(block[: held - FRONT], 64)], axis=0)
    extra = column(block[held - FRONT : held - FRONT + 1], held, 64)
    return jnp.where(lane < 64, full, jnp.where(lane == 64, extra, 0.0))


def plane_at(cores):
    return lax.axis_index("y") * cores + lax.axis_index("c")


def row_parts(rows, enter, leave, bias, head):
    wide = rows.astype(f32)
    low = dot(rows, enter)
    carry = dot((wide * head).astype(bf16), leave, 1, 1)
    return low, carry, jnp.sum(head * (wide * bias + wide), axis=1, keepdims=True)


def parts_kernel(
    cols, cores, table_u, scale, table_i, owner_u, row_u, owner_i, row_i, enter_u, enter_i, leave_u, leave_i,
    bias_u, bias_i, head_u, head_i, send, names,
):
    users = table_u.shape[0]
    part = enter_u.shape[1] // cols
    scales = scale[...].astype(f32)
    eye = iota((users, users), 0) == iota((users, users), 1)
    scales = jnp.sum(jnp.where(eye, scales, 0.0), axis=1, keepdims=True)
    rows = (table_u[...].astype(f32) * scales).astype(bf16)
    low_u, carry_u, line_u = row_parts(rows, enter_u[...], leave_u[...], bias_u[...], head_u[...])
    low_i, carry_i, line_i = row_parts(table_i[...], enter_i[...], leave_i[...], bias_i[...], head_i[...])
    low = jnp.concatenate([low_u, low_i], axis=0)
    carry = jnp.concatenate([carry_u, carry_i], axis=0)
    line = jnp.concatenate([line_u, line_i], axis=0)
    lane = iota(low.shape, 1)
    packed = []
    for x in range(cols):
        full = jnp.where(lane < part, roll(low, -part * x), roll(carry, part - part * x))
        packed.append(pack(full, line).astype(bf16))
    lists = owner_i.shape[0]
    fill = jnp.zeros((FRONT - 2 * lists - 2, LANES), i32)
    idx = jnp.concatenate([owner_u[...], row_u[...], owner_i[...], row_i[...], fill], axis=0)
    idx = idx.astype(f32).astype(bf16)
    names[...] = idx
    mine = plane_at(cores)
    for p in range(send.shape[0]):
        send[p] = jnp.where(mine == p // cols, packed[p % cols], idx)


def share_kernel(cols, cores, came, send):
    mine = plane_at(cores)
    total = came[mine * cols].astype(f32)
    for x in range(1, cols):
        total = total + came[mine * cols + x].astype(f32)
    total = total.astype(bf16)
    for z in range(send.shape[0]):
        send[z] = total


def pick_kernel(cols, cores, depth, users, held, lists, came, names, pick, pick_t):
    mine = plane_at(cores)
    peers = came.shape[0] // cols
    imps, span = LANES, depth * held
    keys = []
    for p in range(peers):
        idx = jnp.where(mine == p, names[...], came[p * cols]).astype(f32).astype(i32)
        owner = jnp.concatenate([idx[0:1], idx[2 : 2 + lists]], axis=0)
        row = jnp.concatenate([idx[1:2], idx[2 + lists : 2 + 2 * lists] + users], axis=0)
        chip = owner // cores
        at = (chip // depth) * cores + owner % cores
        key = jnp.where(at == mine, (chip % depth) * held + row, -1)
        keys.append(jnp.concatenate([key, jnp.full((8 - key.shape[0], imps), -1, i32)], axis=0))
    ids = iota((span, imps), 0)
    for p in range(peers):
        hit = ids == keys[p][0:1]
        for j in range(1, 1 + lists):
            hit = hit | (ids == keys[p][j : j + 1])
        pick_t[:, p * imps : (p + 1) * imps] = jnp.where(hit, 1.0, 0.0).astype(bf16)
    every = jnp.concatenate(keys, axis=0).astype(f32)
    every = jnp.concatenate([every, jnp.zeros((LANES - every.shape[0], LANES), f32)], axis=0)
    every = jnp.transpose(every).astype(i32)
    ids = iota((imps, span), 1)
    for p in range(peers):
        hit = ids == every[:, 8 * p : 8 * p + 1]
        for j in range(1, 1 + lists):
            hit = hit | (ids == every[:, 8 * p + j : 8 * p + j + 1])
        pick[p * imps : (p + 1) * imps, :] = jnp.where(hit, 1.0, 0.0).astype(bf16)


def fetch_kernel(held, came, pick, send):
    table = [unpack(came[z].astype(f32), held) for z in range(came.shape[0])]
    table = jnp.concatenate(table, axis=0).astype(bf16)
    send[...] = dot(pick[...], table).astype(bf16)


def loss_kernel(cols, part, came, labels, send):
    own = came.shape[1]
    peers = came.shape[0] // cols
    lane = iota((own, LANES), 1)
    sums = []
    logits = None
    for x in range(cols):
        total = came[x].astype(f32)
        for p in range(1, peers):
            total = total + came[p * cols + x].astype(f32)
        sums.append(total)
        term = jnp.where(lane < part, total * roll(total, -part), 0.0)
        if x == 0:
            term = term + jnp.where(lane == 2 * part, total, 0.0)
        logits = term if logits is None else logits + term
    logits = jnp.sum(logits, axis=1, keepdims=True)
    target = column(labels[...], own, lax.axis_index("x") * own)
    grad = loss_scale * (1.0 / (1.0 + jnp.exp(-logits)) - target)
    for x in range(cols):
        back = (grad * jnp.where(lane == 2 * part, 1.0, sums[x])).astype(bf16)
        for p in range(peers):
            send[p * cols + x] = back


def back_kernel(held, came, pick_t, send):
    sums = dot(pick_t[...], came[...])
    for z in range(send.shape[0]):
        full = sums[z * held : (z + 1) * held]
        send[z] = pack(full, full[:, 64:65]).astype(bf16)


def total_kernel(came, send):
    total = came[0].astype(f32)
    for z in range(1, came.shape[0]):
        total = total + came[z].astype(f32)
    total = total.astype(bf16)
    for x in range(send.shape[0]):
        send[x] = total


def grad_kernel(
    part, users, held, came, enter_u, enter_i, leave_u, leave_i, bias_u, bias_i, head_u, head_i, out_u, out_i
):
    lane = iota((held, LANES), 1)
    low = carry = jnp.zeros((held, LANES), f32)
    for x in range(came.shape[0]):
        full = unpack(came[x].astype(f32), held)
        if x == 0:
            line = full[:, 64:65]
        here = (lane >= part * x) & (lane < part * (x + 1))
        low = jnp.where(here, roll(full, part * x), low)
        carry = jnp.where(here, roll(full, part * x - part), carry)
    low, carry = low.astype(bf16), carry.astype(bf16)
    for out, a, b, enter, leave, bias, head in (
        (out_u, 0, users, enter_u, leave_u, bias_u, head_u),
        (out_i, users, held, enter_i, leave_i, bias_i, head_i),
    ):
        hidden = dot(low[a:b], leave[...])
        out[...] = head[...] * (hidden + line[a:b] * (bias[...] + 1.0)) + dot(carry[a:b], enter[...], 1, 1)


def call(kernel, outs, flops, bytes_accessed, *args, fetch=False):
    many = isinstance(outs, list)
    spec = pl.BlockSpec(memory_space=pltpu.VMEM)
    if fetch:
        return pl.pallas_call(
            kernel,
            out_shape=outs,
            grid=(1,),
            in_specs=[pl.BlockSpec(a.shape, lambda i: (0, 0)) for a in args],
            out_specs=[spec] * len(outs) if many else spec,
            compiler_params=pltpu.CompilerParams(vmem_limit_bytes=60 * 1024 * 1024),
            cost_estimate=pl.CostEstimate(flops=flops, bytes_accessed=bytes_accessed, transcendentals=0),
        )(*args)
    return pl.pallas_call(
        kernel,
        out_shape=outs,
        in_specs=[spec] * len(args),
        out_specs=[spec] * len(outs) if many else spec,
        compiler_params=pltpu.CompilerParams(vmem_limit_bytes=40 * 1024 * 1024),
        cost_estimate=pl.CostEstimate(flops=flops, bytes_accessed=bytes_accessed, transcendentals=0),
    )(*args)


def swap(value, axes):
    return lax.all_to_all(value, axes, split_axis=0, concat_axis=0, tiled=True)


def body(
    user_table,
    user_scale,
    item_table,
    user_owner,
    user_row,
    item_owner,
    item_row,
    labels,
    enter_user,
    enter_item,
    leave_user,
    leave_item,
    bias_user,
    bias_item,
    head_user,
    head_item,
):
    cols, depth, cores = lax.axis_size("x"), lax.axis_size("z"), lax.axis_size("c")
    peers = lax.axis_size("y") * cores
    users, items = user_table.shape[0], item_table.shape[0]
    imps, lists = item_row.shape
    part = enter_user.shape[1] // cols
    held = users + items
    span = depth * held
    own = imps // cols
    shape = jax.ShapeDtypeStruct
    weights = (enter_user, enter_item, leave_user, leave_item) + tuple(
        v[None] for v in (bias_user, bias_item, head_user, head_item)
    )

    send, names = call(
        lambda *refs: parts_kernel(cols, cores, *refs),
        [shape((peers * cols, FRONT, LANES), bf16), shape((FRONT, LANES), bf16)],
        20_000_000, 2_500_000,
        user_table, user_scale[None], item_table, user_owner.T, user_row[None], item_owner.T, item_row.T, *weights, fetch=True,
    )
    came = swap(send, BLOCK)
    send = call(
        lambda *refs: share_kernel(cols, cores, *refs), shape((depth, FRONT, LANES), bf16), 100_000, 200_000, came
    )
    table = swap(send, "z")
    pick, pick_t = call(
        lambda *refs: pick_kernel(cols, cores, depth, users, held, lists, *refs),
        [shape((peers * imps, span), bf16), shape((span, peers * imps), bf16)],
        100_000_000, 10_000_000,
        came, names,
    )
    send = call(
        lambda *refs: fetch_kernel(held, *refs), shape((peers * imps, LANES), bf16), 200_000_000, 1_500_000, table, pick
    )
    came = swap(send.reshape(peers * cols, own, LANES), BLOCK)
    send = call(
        lambda *refs: loss_kernel(cols, part, *refs),
        shape((peers * cols, own, LANES), bf16), 1_000_000, 500_000,
        came, labels[None],
    )
    came = swap(send, BLOCK)
    send = call(
        lambda *refs: back_kernel(held, *refs),
        shape((depth, FRONT, LANES), bf16), 200_000_000, 1_500_000,
        came.reshape(peers * imps, LANES), pick_t,
    )
    came = swap(send, "z")
    send = call(total_kernel, shape((cols, FRONT, LANES), bf16), 100_000, 200_000, came)
    came = swap(send, "x")
    user_grad, item_grad = call(
        lambda *refs: grad_kernel(part, users, held, *refs),
        [shape(user_table.shape, f32), shape(item_table.shape, f32)],
        20_000_000, 2_500_000,
        came, *weights,
    )
    return (user_grad, item_grad)


def solution(mesh):
    cols = mesh.shape["col"]
    cells = mesh.devices.reshape(-1, 16, 2, cols)
    fine = Mesh(cells, ("y", "z", "c", "x"))
    return jax.shard_map(
        body,
        mesh=fine,
        in_specs=(
            P(EMB, "x"),
            P(EMB),
            P(EMB, "x"),
            P(EMB, None),
            P(EMB),
            P(EMB, None),
            P(EMB, None),
            P(EMB),
            P("x", None),
            P("x", None),
            P(None, "x"),
            P(None, "x"),
            P("x"),
            P("x"),
            P("x"),
            P("x"),
        ),
        out_specs=(P(EMB, "x"), P(EMB, "x")),
        check_vma=False,
    )
```

```python
import jax
import jax.numpy as jnp
from jax import lax
from jax.experimental import pallas as pl
from jax.experimental.pallas import tpu as pltpu
from jax.sharding import Mesh, PartitionSpec as P

loss_scale = 128.0
bf16 = jnp.bfloat16
f32 = jnp.float32
i32 = jnp.int32
EMB = ("y", "z", "c")
BLOCK = ("y", "x")
LANES = 128
FRONT = 24


def dot(a, b, ca=1, cb=0):
    return lax.dot_general(a, b, (((ca,), (cb,)), ((), ())), preferred_element_type=f32)


def iota(shape, axis):
    return lax.broadcasted_iota(i32, shape, axis)


def roll(value, shift):
    shift = shift % LANES
    return pltpu.roll(value, shift, 1) if shift else value


def column(row, rows, first=0):
    wide = (rows, row.shape[1])
    hit = iota(wide, 1) == iota(wide, 0) + first
    return jnp.sum(jnp.where(hit, row, 0.0), axis=1, keepdims=True)


def pack(full, extra):
    held = full.shape[0]
    lane = iota((held, LANES), 1)
    line = jnp.sum(jnp.where(lane == iota((held, LANES), 0) + 64, extra, 0.0), axis=0, keepdims=True)
    tail = jnp.where(iota((2 * FRONT - held, LANES), 0) == 0, line, 0.0)
    right = jnp.concatenate([roll(full[FRONT:], 64), tail], axis=0)
    return jnp.where(lane[:FRONT] < 64, full[:FRONT], right)


def unpack(block, held):
    lane = iota((held, LANES), 1)
    full = jnp.concatenate([block, roll(block[: held - FRONT], 64)], axis=0)
    extra = column(block[held - FRONT : held - FRONT + 1], held, 64)
    return jnp.where(lane < 64, full, jnp.where(lane == 64, extra, 0.0))


def row_parts(rows, enter, leave, bias, head):
    wide = rows.astype(f32)
    low = dot(rows, enter)
    carry = dot((wide * head).astype(bf16), leave, 1, 1)
    return low, carry, jnp.sum(head * (wide * bias + wide), axis=1, keepdims=True)


def turn(column):
    eye = iota((LANES, LANES), 0) == iota((LANES, LANES), 1)
    return jnp.sum(jnp.where(eye, column, 0.0), axis=0, keepdims=True)


def parts_kernel(
    cols, table_u, scale, table_i, owner_u, row_u, owner_i, row_i, labels, enter_u, enter_i, leave_u, leave_i,
    bias_u, bias_i, head_u, head_i, send, names,
):
    users = table_u.shape[0]
    part = enter_u.shape[1] // cols
    scales = column(scale[...].astype(f32), users)
    rows = (table_u[...].astype(f32) * scales).astype(bf16)
    low_u, carry_u, line_u = row_parts(rows, enter_u[...], leave_u[...], bias_u[...], head_u[...])
    low_i, carry_i, line_i = row_parts(table_i[...], enter_i[...], leave_i[...], bias_i[...], head_i[...])
    low = jnp.concatenate([low_u, low_i], axis=0)
    carry = jnp.concatenate([carry_u, carry_i], axis=0)
    line = jnp.concatenate([line_u, line_i], axis=0)
    lane = iota(low.shape, 1)
    packed = []
    for x in range(cols):
        full = jnp.where(lane < part, roll(low, -part * x), roll(carry, part - part * x))
        packed.append(pack(full, line).astype(bf16))
    names_now = [owner_u[...], row_u[...], owner_i[...], row_i[...]]
    rest = labels[...]
    targets = []
    for _ in range(3):
        piece = rest.astype(bf16).astype(f32)
        targets.append(piece)
        rest = rest - piece
    idx = jnp.concatenate([v.astype(f32) for v in names_now] + targets, axis=0)
    idx = jnp.concatenate([idx, jnp.zeros((FRONT - idx.shape[0], LANES), f32)], axis=0).astype(bf16)
    names[...] = idx
    mine = lax.axis_index("y")
    for p in range(send.shape[0]):
        send[p] = jnp.where(mine == p // cols, packed[p % cols], idx)


def share_kernel(cols, came, send):
    mine = lax.axis_index("y")
    total = came[mine * cols].astype(f32)
    for x in range(1, cols):
        total = total + came[mine * cols + x].astype(f32)
    total = total.astype(bf16)
    for z in range(send.shape[0]):
        send[z] = total


def pick_kernel(cols, cores, depth, users, held, lists, came, names, pick, pick_t, labels):
    mine, core = lax.axis_index("y"), lax.axis_index("c")
    peers = came.shape[0] // cols
    imps, span = LANES, cores * depth * held
    keys, targets = [], []
    for p in range(peers):
        block = jnp.where(mine == p, names[...], came[p * cols]).astype(f32)
        idx = block.astype(i32)
        owner = jnp.concatenate([idx[0:1], idx[2 : 2 + lists]], axis=0)
        row = jnp.concatenate([idx[1:2], idx[2 + lists : 2 + 2 * lists] + users], axis=0)
        chip = owner // cores
        side = jnp.where(owner % cores == core, 0, depth)
        key = jnp.where(chip // depth == mine, (side + chip % depth) * held + row, -1)
        keys.append(jnp.concatenate([key, jnp.full((8 - key.shape[0], imps), -1, i32)], axis=0))
        first = 2 + 2 * lists
        targets.append((block[first : first + 1] + block[first + 1 : first + 2]) + block[first + 2 : first + 3])
    labels[...] = jnp.concatenate(targets + [jnp.zeros((8 - peers, LANES), f32)], axis=0)
    ids = iota((span, imps), 0)
    for p in range(peers):
        hit = ids == keys[p][0:1]
        for j in range(1, 1 + lists):
            hit = hit | (ids == keys[p][j : j + 1])
        pick_t[:, p * imps : (p + 1) * imps] = jnp.where(hit, 1.0, 0.0).astype(bf16)
    every = jnp.concatenate(keys, axis=0).astype(f32)
    every = jnp.concatenate([every, jnp.zeros((LANES - every.shape[0], LANES), f32)], axis=0)
    every = jnp.transpose(every).astype(i32)
    ids = iota((imps, span), 1)
    for p in range(peers):
        hit = ids == every[:, 8 * p : 8 * p + 1]
        for j in range(1, 1 + lists):
            hit = hit | (ids == every[:, 8 * p + j : 8 * p + j + 1])
        pick[p * imps : (p + 1) * imps, :] = jnp.where(hit, 1.0, 0.0).astype(bf16)


def fetch_kernel(held, mine, other, pick, send):
    table = [unpack(side[z].astype(f32), held) for side in (mine, other) for z in range(mine.shape[0])]
    table = jnp.concatenate(table, axis=0).astype(bf16)
    got = dot(pick[...], table)
    half = got.shape[0] // 2
    both = jnp.where(iota((half, LANES), 1) < 64, got[:half], roll(got[half:], 64))
    blocks = got.shape[0] // LANES
    lines = [turn(got[b * LANES : (b + 1) * LANES, 64:65]) for b in range(blocks)]
    lines.append(jnp.zeros((send.shape[1] - half - blocks, LANES), f32))
    block = jnp.concatenate([both] + lines, axis=0).astype(bf16)
    for y in range(send.shape[0]):
        send[y] = block


def logit_kernel(part, came, send, sums):
    total = came[0].astype(f32)
    for y in range(1, came.shape[0]):
        total = total + came[y].astype(f32)
    half = sums.shape[0]
    lines = total[half:]
    total = total[:half]
    sums[...] = total
    lane = iota((half, LANES), 1)
    product = total * roll(total, -part)
    left = jnp.sum(jnp.where(lane < part, product, 0.0), axis=1, keepdims=True)
    right = jnp.sum(jnp.where((lane >= 64) & (lane < 64 + part), product, 0.0), axis=1, keepdims=True)
    rows = [turn(side[b * LANES : (b + 1) * LANES]) for side in (left, right) for b in range(half // LANES)]
    rows.append(jnp.zeros((send.shape[1] - len(rows), LANES), f32))
    rows = jnp.concatenate(rows, axis=0) + lines * (1.0 / send.shape[0])
    for x in range(send.shape[0]):
        send[x] = rows


def back_kernel(held, came, labels, sums, pick_t, keep, give):
    logits = came[0]
    for x in range(1, came.shape[0]):
        logits = logits + came[x]
    grad = loss_scale * (1.0 / (1.0 + jnp.exp(-logits)) - labels[...])
    half = sums.shape[0]
    blocks = half // LANES
    lane = iota((half, LANES), 1)
    cols = [column(grad[b : b + 1], LANES) for b in range(2 * blocks)]
    left, right = jnp.concatenate(cols[:blocks], axis=0), jnp.concatenate(cols[blocks:], axis=0)
    scaled = sums[...] * jnp.where(lane < 64, left, right)
    sides = [
        jnp.where(lane < 64, value, jnp.where(lane == 64, line, 0.0))
        for value, line in ((scaled, left), (roll(scaled, 64), right))
    ]
    back = dot(pick_t[...], jnp.concatenate(sides, axis=0).astype(bf16))
    depth = keep.shape[0]
    for z in range(2 * depth):
        full = back[z * held : (z + 1) * held]
        block = pack(full, full[:, 64:65])
        if z < depth:
            keep[z] = block
        else:
            give[z - depth] = block.astype(bf16)


def join_kernel(keep, came, send):
    send[...] = (keep[...] + came[...].astype(f32)).astype(bf16)


def total_kernel(came, send):
    total = came[0].astype(f32)
    for z in range(1, came.shape[0]):
        total = total + came[z].astype(f32)
    total = total.astype(bf16)
    for x in range(send.shape[0]):
        send[x] = total


def grad_kernel(
    part, users, held, came, enter_u, enter_i, leave_u, leave_i, bias_u, bias_i, head_u, head_i, out_u, out_i
):
    lane = iota((held, LANES), 1)
    low = carry = jnp.zeros((held, LANES), f32)
    for x in range(came.shape[0]):
        full = unpack(came[x].astype(f32), held)
        if x == 0:
            line = full[:, 64:65]
        here = (lane >= part * x) & (lane < part * (x + 1))
        low = jnp.where(here, roll(full, part * x), low)
        carry = jnp.where(here, roll(full, part * x - part), carry)
    low, carry = low.astype(bf16), carry.astype(bf16)
    for out, a, b, enter, leave, bias, head in (
        (out_u, 0, users, enter_u, leave_u, bias_u, head_u),
        (out_i, users, held, enter_i, leave_i, bias_i, head_i),
    ):
        hidden = dot(low[a:b], leave[...])
        out[...] = head[...] * (hidden + line[a:b] * (bias[...] + 1.0)) + dot(carry[a:b], enter[...], 1, 1)


def call(kernel, outs, flops, bytes_accessed, *args, fetch=False):
    many = isinstance(outs, list)
    spec = pl.BlockSpec(memory_space=pltpu.VMEM)
    if fetch:
        return pl.pallas_call(
            kernel,
            out_shape=outs,
            grid=(1,),
            in_specs=[pl.BlockSpec(a.shape, lambda i: (0, 0)) for a in args],
            out_specs=[spec] * len(outs) if many else spec,
            compiler_params=pltpu.CompilerParams(vmem_limit_bytes=60 * 1024 * 1024),
            cost_estimate=pl.CostEstimate(flops=flops, bytes_accessed=bytes_accessed, transcendentals=0),
        )(*args)
    return pl.pallas_call(
        kernel,
        out_shape=outs,
        in_specs=[spec] * len(args),
        out_specs=[spec] * len(outs) if many else spec,
        compiler_params=pltpu.CompilerParams(vmem_limit_bytes=40 * 1024 * 1024),
        cost_estimate=pl.CostEstimate(flops=flops, bytes_accessed=bytes_accessed, transcendentals=0),
    )(*args)


def swap(value, axes):
    return lax.all_to_all(value, axes, split_axis=0, concat_axis=0, tiled=True)


def body(
    user_table,
    user_scale,
    item_table,
    user_owner,
    user_row,
    item_owner,
    item_row,
    labels,
    enter_user,
    enter_item,
    leave_user,
    leave_item,
    bias_user,
    bias_item,
    head_user,
    head_item,
):
    cols, depth, cores, peers = (lax.axis_size(a) for a in ("x", "z", "c", "y"))
    users, items = user_table.shape[0], item_table.shape[0]
    imps, lists = item_row.shape
    part = enter_user.shape[1] // cols
    held = users + items
    span = cores * depth * held
    mass = peers * imps
    half = mass // 2
    pair = [(0, 1), (1, 0)]
    shape = jax.ShapeDtypeStruct
    weights = (enter_user, enter_item, leave_user, leave_item) + tuple(
        v[None] for v in (bias_user, bias_item, head_user, head_item)
    )

    send, names = call(
        lambda *refs: parts_kernel(cols, *refs),
        [shape((peers * cols, FRONT, LANES), bf16), shape((FRONT, LANES), bf16)],
        20_000_000, 2_500_000,
        user_table, user_scale[None], item_table, user_owner.T, user_row[None], item_owner.T, item_row.T, labels[None],
        *weights, fetch=True,
    )
    came = swap(send, BLOCK)
    send = call(lambda *refs: share_kernel(cols, *refs), shape((depth, FRONT, LANES), bf16), 100_000, 200_000, came)
    table = swap(send, "z")
    pick, pick_t, targets = call(
        lambda *refs: pick_kernel(cols, cores, depth, users, held, lists, *refs),
        [shape((mass, span), bf16), shape((span, mass), bf16), shape((8, LANES), f32)],
        100_000_000, 10_000_000,
        came, names,
    )
    table, pick, pick_t, targets = lax.optimization_barrier((table, pick, pick_t, targets))
    other = lax.ppermute(table, "c", pair)
    send = call(
        lambda *refs: fetch_kernel(held, *refs),
        shape((peers, half + 8, LANES), bf16), 200_000_000, 1_500_000,
        table, other, pick,
    )
    came = swap(send, "y")
    send, sums = call(
        lambda *refs: logit_kernel(part, *refs),
        [shape((cols, 8, LANES), f32), shape((half, LANES), f32)], 1_000_000, 500_000,
        came,
    )
    came = swap(send, "x")
    keep, give = call(
        lambda *refs: back_kernel(held, *refs),
        [shape((depth, FRONT, LANES), f32), shape((depth, FRONT, LANES), bf16)], 200_000_000, 1_500_000,
        came, targets, sums, pick_t,
    )
    send = call(
        join_kernel, shape((depth, FRONT, LANES), bf16), 100_000, 400_000, keep, lax.ppermute(give, "c", pair)
    )
    came = swap(send, "z")
    send = call(total_kernel, shape((cols, FRONT, LANES), bf16), 100_000, 200_000, came)
    came = swap(send, "x")
    user_grad, item_grad = call(
        lambda *refs: grad_kernel(part, users, held, *refs),
        [shape(user_table.shape, f32), shape(item_table.shape, f32)],
        20_000_000, 2_500_000,
        came, *weights,
    )
    return (user_grad, item_grad)


def solution(mesh):
    cols = mesh.shape["col"]
    cells = mesh.devices.reshape(-1, 16, 2, cols)
    fine = Mesh(cells, ("y", "z", "c", "x"))
    return jax.shard_map(
        body,
        mesh=fine,
        in_specs=(
            P(EMB, "x"),
            P(EMB),
            P(EMB, "x"),
            P(EMB, None),
            P(EMB),
            P(EMB, None),
            P(EMB, None),
            P(EMB),
            P("x", None),
            P("x", None),
            P(None, "x"),
            P(None, "x"),
            P("x"),
            P("x"),
            P("x"),
            P("x"),
        ),
        out_specs=(P(EMB, "x"), P(EMB, "x")),
        check_vma=False,
    )
```

```python
import jax
import jax.numpy as jnp
from jax import lax
from jax.experimental import pallas as pl
from jax.experimental.pallas import tpu as pltpu
from jax.sharding import Mesh, PartitionSpec as P

loss_scale = 128.0
bf16 = jnp.bfloat16
f32 = jnp.float32
i32 = jnp.int32
EMB = ("y", "z", "c")
BLOCK = ("y", "c", "x")
LANES = 128
TILES = 3
SLOTS = 4


def dot(a, b, ca=1, cb=0):
    return lax.dot_general(a, b, (((ca,), (cb,)), ((), ())), preferred_element_type=f32)


def iota(shape, axis):
    return lax.broadcasted_iota(i32, shape, axis)


def roll(value, shift):
    shift = shift % LANES
    return pltpu.roll(value, shift, 1) if shift else value


def column(row, rows, first=0):
    wide = (rows, row.shape[1])
    hit = iota(wide, 1) == iota(wide, 0) + first
    return jnp.sum(jnp.where(hit, row, 0.0), axis=1, keepdims=True)


def row_parts(rows, enter, leave, bias, head):
    wide = rows.astype(f32)
    low = dot(rows, enter)
    carry = dot((wide * head).astype(bf16), leave, 1, 1)
    return low, carry, jnp.sum(head * (wide * bias + wide), axis=1, keepdims=True)


def split(value):
    return [value[8 * t : 8 * t + 8] for t in range(TILES)]


def unit(value, octet):
    if value == 8:
        return (octet * SLOTS + 2, 2) if octet < 4 else (3, 2)
    q = octet + 5 * (value // 4)
    return (value % 4) * SLOTS + q % SLOTS, q // SLOTS


def exchange(blocks):
    group = iota((8, LANES), 1) // 8
    for bit in (1, 2, 4, 8):
        low = (group & bit) == 0
        after = list(blocks)
        for z in range(16):
            if z & bit == 0:
                a, b = blocks[z], blocks[z | bit]
                after[z] = [jnp.where(low, a[t], roll(b[t], 8 * bit)) for t in range(TILES)]
                after[z | bit] = [jnp.where(low, roll(a[t], -8 * bit), b[t]) for t in range(TILES)]
        blocks = after
    return blocks


def parts_kernel(
    table_u, scale, table_i, owner_u, row_u, owner_i, row_i, labels, enter_u, enter_i, leave_u, leave_i,
    bias_u, bias_i, head_u, head_i, send,
):
    users = table_u.shape[0]
    scales = column(scale[...].astype(f32), users)
    rows = (table_u[...].astype(f32) * scales).astype(bf16)
    low_u, carry_u, line_u = row_parts(rows, enter_u[...], leave_u[...], bias_u[...], head_u[...])
    low_i, carry_i, line_i = row_parts(table_i[...], enter_i[...], leave_i[...], bias_i[...], head_i[...])
    octets = [low_u] + [low_i[8 * o : 8 * o + 8] for o in range(4)]
    octets += [carry_u] + [carry_i[8 * o : 8 * o + 8] for o in range(4)]
    lines = [line_u] + [line_i[8 * o : 8 * o + 8] for o in range(4)]
    lane = iota((8, LANES), 1)
    octets = [roll(v, q) for q, v in enumerate(octets)]
    flat = jnp.zeros((8, LANES), f32)
    for o, line in enumerate(lines):
        flat = jnp.where(lane == (32 * o + 10 if o < 4 else 11), line, flat)
    parts = [v[...].astype(f32) for v in (owner_u, row_u, owner_i, row_i)]
    rest = labels[...]
    for _ in range(3):
        piece = rest.astype(bf16).astype(f32)
        parts.append(piece)
        rest = rest - piece
    names = jnp.concatenate(parts + [jnp.zeros((3, LANES), f32)], axis=0)
    mine = lax.axis_index("x")
    share = names[0:4]
    for x in range(1, 4):
        share = jnp.where(mine == x, names[4 * x : 4 * x + 4], share)
    moved = roll(share, 16)
    share = jnp.concatenate([v[r : r + 1] for r in range(4) for v in (moved, share)], axis=0)
    flat = jnp.where(lane % 32 < 16, flat, share)
    for p in range(send.shape[0]):
        at = (lane - p) & 31
        tile = jnp.zeros((8, LANES), f32)
        for q, value in enumerate(octets):
            tile = jnp.where(at == q, value, tile)
        send[p] = (roll(tile, -p) + flat).astype(bf16)


def share_kernel(came, send):
    lane = iota((8, LANES), 1)
    planes = []
    for b in range(came.shape[0] // 4):
        total = came[4 * b].astype(f32)
        for x in range(1, 4):
            total = total + came[4 * b + x].astype(f32)
        planes.append(roll(total, b))
    tiles = []
    for t in range(TILES):
        tile = jnp.zeros((8, LANES), f32)
        for sub in range(SLOTS):
            q = SLOTS * t + sub
            at = (lane - q) & 31
            value = jnp.zeros((8, LANES), f32)
            for b, plane in enumerate(planes):
                value = jnp.where(at == b, plane, value)
            tile = tile + roll(value, 8 * sub - q)
        tiles.append(tile)
    block = jnp.concatenate(tiles, axis=0).astype(bf16)
    for z in range(send.shape[0]):
        send[z] = block


def pick_kernel(came, owners, rows, labels):
    blocks = came.shape[0] // 4
    names, targets = [], []
    odd = iota((8, LANES), 0) % 2 == 1
    side = iota((1, LANES), 1) % 32 >= 16
    for b in range(blocks):
        share = [came[4 * b + x].astype(f32) for x in range(4)]
        share = jnp.concatenate([jnp.where(odd, v, roll(v, -16)) for v in share], axis=0)
        block = jnp.concatenate([jnp.where(side, share[r + 1 : r + 2], share[r : r + 1]) for r in range(0, 32, 2)], axis=0)
        names.append(block.astype(i32))
        targets.append((block[10:11] + block[11:12]) + block[12:13])
    labels[...] = jnp.concatenate(targets, axis=0)
    names = jnp.concatenate(names, axis=1)
    mass = names.shape[1]
    ids = iota((LANES, mass), 0)
    tall = iota((32, mass), 0)
    for j in range(5):
        owner = names[j + 1 : j + 2] if j else names[0:1]
        row = names[j + 5 : j + 6] if j else names[1:2]
        y, z, c = owner // 32, (owner // 2) % 16, owner % 2
        owners[j] = jnp.where(ids == z * 8 + y * 2 + c, 1.0, 0.0).astype(bf16)
        if j:
            rows[32 * j - 24 : 32 * j + 8, :] = jnp.where(tall == row, 1.0, 0.0)
        else:
            rows[0:8, :] = jnp.where(tall[:8] == row, 1.0, 0.0)


def fetch_kernel(came, owners, rows, send, sums):
    blocks = exchange([split(came[z].astype(f32)) for z in range(came.shape[0])])

    def table(octets):
        tiles = []
        for w in range(9):
            for o in octets:
                g, t = unit(w, o)
                tiles.append(blocks[g][t])
        return jnp.concatenate(tiles, axis=0).astype(bf16)

    got = dot(table([0]), owners[0])
    mask = rows[0:8, :]
    total = [got[8 * w : 8 * w + 8] * mask for w in range(9)]
    listed = table([1, 2, 3, 4])
    for j in range(1, 5):
        got = dot(listed, owners[j])
        masks = [rows[32 * j - 24 + 8 * o : 32 * j - 16 + 8 * o, :] for o in range(4)]
        for w in range(9):
            for o in range(4):
                at = 8 * (4 * w + o)
                total[w] = total[w] + got[at : at + 8] * masks[o]
    total = [jnp.sum(v, axis=0, keepdims=True) for v in total]
    logits = total[8] * (1.0 / send.shape[0])
    for w in range(4):
        logits = logits + total[w] * total[w + 4]
    sums[...] = jnp.concatenate(total + [jnp.zeros((7, logits.shape[1]), f32)], axis=0)
    logits = jnp.concatenate([logits[:, LANES * b : LANES * (b + 1)] for b in range(8)], axis=0)
    for p in range(send.shape[0]):
        send[p] = logits


def back_kernel(came, labels, sums, owners, rows, send):
    logits = came[0]
    for p in range(1, came.shape[0]):
        logits = logits + came[p]
    grad = loss_scale * (1.0 / (1.0 + jnp.exp(-logits)) - labels[...])
    grad = jnp.concatenate([grad[b : b + 1] for b in range(8)], axis=1)
    back = [grad * sums[w : w + 1, :] for w in range(8)] + [grad]

    def scatter(j, masks):
        tall = jnp.concatenate([mask * value for value in back for mask in masks], axis=0)
        return dot(tall.astype(bf16), owners[j], 1, 1)

    own = scatter(0, [rows[0:8, :]])
    listed = None
    for j in range(1, 5):
        part = scatter(j, [rows[32 * j - 24 + 8 * o : 32 * j - 16 + 8 * o, :] for o in range(4)])
        listed = part if listed is None else listed + part
    empty = jnp.zeros((8, LANES), f32)
    blocks = [[empty] * TILES for _ in range(16)]
    for w in range(9):
        for o in range(5):
            g, t = unit(w, o)
            at = 8 * (4 * w + o - 1)
            blocks[g][t] = listed[at : at + 8] if o else own[8 * w : 8 * w + 8]
    blocks = exchange(blocks)
    for z in range(send.shape[0]):
        send[z] = jnp.concatenate(blocks[z], axis=0).astype(bf16)


def total_kernel(came, send):
    lane = iota((8, LANES), 1)
    total = came[0].astype(f32)
    for z in range(1, came.shape[0]):
        total = total + came[z].astype(f32)
    tiles = split(total)
    values = [roll(tiles[q // SLOTS], q - 8 * (q % SLOTS)) for q in range(SLOTS * TILES)]
    for b in range(send.shape[0] // 4):
        at = (lane - b) & 31
        tile = jnp.zeros((8, LANES), f32)
        for q, value in enumerate(values):
            tile = jnp.where(at == q, value, tile)
        tile = roll(tile, -b).astype(bf16)
        for x in range(4):
            send[4 * b + x] = tile


def grad_kernel(users, came, enter_u, enter_i, leave_u, leave_i, bias_u, bias_i, head_u, head_i, out_u, out_i):
    lane = iota((8, LANES), 1)
    ranks = [jnp.zeros((8, LANES), f32)] * 10
    ats = [(lane - q) & 31 for q in range(10)]
    for p in range(came.shape[0]):
        tile = came[p].astype(f32)
        if p == 0:
            hits = [lane == (32 * o + 10 if o < 4 else 11) for o in range(5)]
            lines = [jnp.sum(jnp.where(hit, tile, 0.0), axis=1, keepdims=True) for hit in hits]
        tile = roll(tile, p)
        for q in range(10):
            ranks[q] = jnp.where(ats[q] == p, tile, ranks[q])
    ranks = [roll(v, -q) for q, v in enumerate(ranks)]
    low = jnp.concatenate(ranks[:5], axis=0)
    carry = jnp.concatenate(ranks[5:], axis=0)
    line = jnp.concatenate(lines, axis=0)
    held = low.shape[0]
    for out, a, b, enter, leave, bias, head in (
        (out_u, 0, users, enter_u, leave_u, bias_u, head_u),
        (out_i, users, held, enter_i, leave_i, bias_i, head_i),
    ):
        hidden = dot(low[a:b].astype(bf16), leave[...])
        back = dot(carry[a:b].astype(bf16), enter[...], 1, 1)
        out[...] = head[...] * (hidden + line[a:b] * (bias[...] + 1.0)) + back


def call(kernel, outs, flops, bytes_accessed, *args, fetch=False):
    many = isinstance(outs, list)
    spec = pl.BlockSpec(memory_space=pltpu.VMEM)
    if fetch:
        return pl.pallas_call(
            kernel,
            out_shape=outs,
            grid=(1,),
            in_specs=[pl.BlockSpec(a.shape, lambda i: (0, 0)) for a in args],
            out_specs=[spec] * len(outs) if many else spec,
            compiler_params=pltpu.CompilerParams(vmem_limit_bytes=60 * 1024 * 1024),
            cost_estimate=pl.CostEstimate(flops=flops, bytes_accessed=bytes_accessed, transcendentals=0),
        )(*args)
    return pl.pallas_call(
        kernel,
        out_shape=outs,
        in_specs=[spec] * len(args),
        out_specs=[spec] * len(outs) if many else spec,
        compiler_params=pltpu.CompilerParams(vmem_limit_bytes=40 * 1024 * 1024),
        cost_estimate=pl.CostEstimate(flops=flops, bytes_accessed=bytes_accessed, transcendentals=0),
    )(*args)


def swap(value, axes):
    return lax.all_to_all(value, axes, split_axis=0, concat_axis=0, tiled=True)


def body(
    user_table,
    user_scale,
    item_table,
    user_owner,
    user_row,
    item_owner,
    item_row,
    labels,
    enter_user,
    enter_item,
    leave_user,
    leave_item,
    bias_user,
    bias_item,
    head_user,
    head_item,
):
    depth = lax.axis_size("z")
    plane = lax.axis_size("y") * lax.axis_size("c") * lax.axis_size("x")
    users = user_table.shape[0]
    mass = labels.shape[0] * lax.axis_size("y") * lax.axis_size("c")
    block = 8 * TILES
    shape = jax.ShapeDtypeStruct
    weights = (enter_user, enter_item, leave_user, leave_item) + tuple(
        v[None] for v in (bias_user, bias_item, head_user, head_item)
    )

    send = call(
        parts_kernel, shape((plane, 8, LANES), bf16), 20_000_000, 2_500_000,
        user_table, user_scale[None], item_table, user_owner.T, user_row[None], item_owner.T, item_row.T, labels[None],
        *weights, fetch=True,
    )
    came = swap(send, BLOCK)
    send = call(share_kernel, shape((depth, block, LANES), bf16), 100_000, 200_000, came)
    table = swap(send, "z")
    owners, rows, targets = call(
        pick_kernel,
        [shape((5, LANES, mass), bf16), shape((136, mass), f32), shape((8, LANES), f32)],
        10_000_000, 3_000_000,
        came,
    )
    send, sums = call(
        fetch_kernel, [shape((plane, 8, LANES), f32), shape((16, mass), f32)], 400_000_000, 3_000_000,
        table, owners, rows,
    )
    came = swap(send, BLOCK)
    send = call(
        back_kernel, shape((depth, block, LANES), bf16), 400_000_000, 3_000_000, came, targets, sums, owners, rows
    )
    came = swap(send, "z")
    send = call(total_kernel, shape((plane, 8, LANES), bf16), 100_000, 200_000, came)
    came = swap(send, BLOCK)
    user_grad, item_grad = call(
        lambda *refs: grad_kernel(users, *refs),
        [shape(user_table.shape, f32), shape(item_table.shape, f32)],
        20_000_000, 2_500_000,
        came, *weights,
    )
    return (user_grad, item_grad)


def solution(mesh):
    cols = mesh.shape["col"]
    cells = mesh.devices.reshape(-1, 16, 2, cols)
    fine = Mesh(cells, ("y", "z", "c", "x"))
    return jax.shard_map(
        body,
        mesh=fine,
        in_specs=(
            P(EMB, "x"),
            P(EMB),
            P(EMB, "x"),
            P(EMB, None),
            P(EMB),
            P(EMB, None),
            P(EMB, None),
            P(EMB),
            P("x", None),
            P("x", None),
            P(None, "x"),
            P(None, "x"),
            P("x"),
            P("x"),
            P("x"),
            P("x"),
        ),
        out_specs=(P(EMB, "x"), P(EMB, "x")),
        check_vma=False,
    )
```

```python
import jax
import jax.numpy as jnp
from jax import lax
from jax.experimental import pallas as pl
from jax.experimental.pallas import tpu as pltpu
from jax.sharding import Mesh, PartitionSpec as P

loss_scale = 128.0
bf16 = jnp.bfloat16
f32 = jnp.float32
i32 = jnp.int32
EMB = ("y", "z", "c")
BLOCK = ("y", "c", "x")
LANES = 128
TILES = 3
SLOTS = 4


def dot(a, b, ca=1, cb=0):
    return lax.dot_general(a, b, (((ca,), (cb,)), ((), ())), preferred_element_type=f32)


def iota(shape, axis):
    return lax.broadcasted_iota(i32, shape, axis)


def roll(value, shift):
    shift = shift % LANES
    return pltpu.roll(value, shift, 1) if shift else value


def column(row, rows, first=0):
    wide = (rows, row.shape[1])
    hit = iota(wide, 1) == iota(wide, 0) + first
    return jnp.sum(jnp.where(hit, row, 0.0), axis=1, keepdims=True)


def row_parts(rows, enter, leave, bias, head):
    wide = rows.astype(f32)
    low = dot(rows, enter)
    carry = dot((wide * head).astype(bf16), leave, 1, 1)
    return low, carry, jnp.sum(head * (wide * bias + wide), axis=1, keepdims=True)


def split(value):
    return [value[8 * t : 8 * t + 8] for t in range(TILES)]


def unit(value, octet):
    if value == 8:
        return (octet * SLOTS + 2, 2) if octet < 4 else (3, 2)
    q = octet + 5 * (value // 4)
    return (value % 4) * SLOTS + q % SLOTS, q // SLOTS


def exchange(blocks):
    group = iota((8, LANES), 1) // 8
    for bit in (1, 2, 4, 8):
        low = (group & bit) == 0
        after = list(blocks)
        for z in range(16):
            if z & bit == 0:
                a, b = blocks[z], blocks[z | bit]
                after[z] = [jnp.where(low, a[t], roll(b[t], 8 * bit)) for t in range(TILES)]
                after[z | bit] = [jnp.where(low, roll(a[t], -8 * bit), b[t]) for t in range(TILES)]
        blocks = after
    return blocks


def parts_kernel(
    table_u, scale, table_i, owner_u, row_u, owner_i, row_i, labels, enter_u, enter_i, leave_u, leave_i,
    bias_u, bias_i, head_u, head_i, send,
):
    users = table_u.shape[0]
    scales = column(scale[...].astype(f32), users)
    rows = (table_u[...].astype(f32) * scales).astype(bf16)
    low_u, carry_u, line_u = row_parts(rows, enter_u[...], leave_u[...], bias_u[...], head_u[...])
    low_i, carry_i, line_i = row_parts(table_i[...], enter_i[...], leave_i[...], bias_i[...], head_i[...])
    octets = [low_u] + [low_i[8 * o : 8 * o + 8] for o in range(4)]
    octets += [carry_u] + [carry_i[8 * o : 8 * o + 8] for o in range(4)]
    lines = [line_u] + [line_i[8 * o : 8 * o + 8] for o in range(4)]
    lane = iota((8, LANES), 1)
    octets = [roll(v, q) for q, v in enumerate(octets)]
    flat = jnp.zeros((8, LANES), f32)
    for o, line in enumerate(lines):
        flat = jnp.where(lane == (32 * o + 10 if o < 4 else 11), line, flat)
    parts = [v[...].astype(f32) for v in (owner_u, row_u, owner_i, row_i)]
    rest = labels[...]
    for _ in range(3):
        piece = rest.astype(bf16).astype(f32)
        parts.append(piece)
        rest = rest - piece
    names = jnp.concatenate(parts + [jnp.zeros((3, LANES), f32)], axis=0)
    mine = lax.axis_index("x")
    share = names[0:4]
    for x in range(1, 4):
        share = jnp.where(mine == x, names[4 * x : 4 * x + 4], share)
    moved = roll(share, 16)
    share = jnp.concatenate([v[r : r + 1] for r in range(4) for v in (moved, share)], axis=0)
    flat = jnp.where(lane % 32 < 16, flat, share)
    for p in range(send.shape[0]):
        at = (lane - p) & 31
        tile = jnp.zeros((8, LANES), f32)
        for q, value in enumerate(octets):
            tile = jnp.where(at == q, value, tile)
        send[p] = (roll(tile, -p) + flat).astype(bf16)


def share_kernel(came, send):
    lane = iota((8, LANES), 1)
    planes = []
    for b in range(came.shape[0] // 4):
        total = came[4 * b].astype(f32)
        for x in range(1, 4):
            total = total + came[4 * b + x].astype(f32)
        planes.append(roll(total, b))
    tiles = []
    for t in range(TILES):
        tile = jnp.zeros((8, LANES), f32)
        for sub in range(SLOTS):
            q = SLOTS * t + sub
            at = (lane - q) & 31
            value = jnp.zeros((8, LANES), f32)
            for b, plane in enumerate(planes):
                value = jnp.where(at == b, plane, value)
            tile = tile + roll(value, 8 * sub - q)
        tiles.append(tile)
    block = jnp.concatenate(tiles, axis=0).astype(bf16)
    for z in range(send.shape[0]):
        send[z] = block


def pick_kernel(came, owners, rows, labels):
    blocks = came.shape[0] // 4
    names, targets = [], []
    odd = iota((8, LANES), 0) % 2 == 1
    side = iota((1, LANES), 1) % 32 >= 16
    for b in range(blocks):
        share = [came[4 * b + x].astype(f32) for x in range(4)]
        share = jnp.concatenate([jnp.where(odd, v, roll(v, -16)) for v in share], axis=0)
        block = jnp.concatenate([jnp.where(side, share[r + 1 : r + 2], share[r : r + 1]) for r in range(0, 32, 2)], axis=0)
        names.append(block.astype(i32))
        targets.append((block[10:11] + block[11:12]) + block[12:13])
    labels[...] = jnp.concatenate(targets, axis=0)
    names = jnp.concatenate(names, axis=1)
    mass = names.shape[1]
    ids = iota((LANES, mass), 0)
    tall = iota((16, mass), 0)
    for j in range(5):
        owner = names[j + 1 : j + 2] if j else names[0:1]
        row = names[j + 5 : j + 6] if j else names[1:2]
        y, z, c = owner // 32, (owner // 2) % 16, owner % 2
        at = z * 8 + y * 2 + c
        if j:
            for side in range(2):
                hit = ids == jnp.where(row // 16 == side, at, -1)
                owners[2 * j - 1 + side] = jnp.where(hit, 1.0, 0.0).astype(bf16)
            rows[16 * j - 8 : 16 * j + 8, :] = jnp.where(tall == row % 16, 1.0, 0.0)
        else:
            owners[0] = jnp.where(ids == at, 1.0, 0.0).astype(bf16)
            rows[0:8, :] = jnp.where(tall[:8] == row, 1.0, 0.0)


def fetch_kernel(came, owners, rows, send, sums):
    blocks = exchange([split(came[z].astype(f32)) for z in range(came.shape[0])])

    def table(octets):
        tiles = []
        for w in range(9):
            for o in octets:
                g, t = unit(w, o)
                tiles.append(blocks[g][t])
        return jnp.concatenate(tiles, axis=0).astype(bf16)

    got = dot(table([0]), owners[0])
    mask = rows[0:8, :]
    total = [got[8 * w : 8 * w + 8] * mask for w in range(9)]
    listed = jnp.concatenate([table([1, 2]), table([3, 4])], axis=1)
    for j in range(1, 5):
        got = dot(listed, jnp.concatenate([owners[2 * j - 1], owners[2 * j]], axis=0))
        masks = [rows[16 * j - 8 + 8 * o : 16 * j + 8 * o, :] for o in range(2)]
        for w in range(9):
            for o in range(2):
                at = 8 * (2 * w + o)
                total[w] = total[w] + got[at : at + 8] * masks[o]
    total = [jnp.sum(v, axis=0, keepdims=True) for v in total]
    first = lax.axis_index("y") + lax.axis_index("c") + lax.axis_index("x") == 0
    logits = jnp.where(first, total[8], 0.0)
    for w in range(4):
        logits = logits + total[w] * total[w + 4]
    sums[...] = jnp.concatenate(total + [jnp.zeros((7, logits.shape[1]), f32)], axis=0)
    logits = jnp.concatenate([logits[:, LANES * b : LANES * (b + 1)] for b in range(8)], axis=0)
    logits = logits.astype(bf16)
    for p in range(send.shape[0]):
        send[p] = logits


def back_kernel(came, labels, sums, owners, rows, send):
    logits = came[0].astype(f32)
    for p in range(1, came.shape[0]):
        logits = logits + came[p].astype(f32)
    grad = loss_scale * (1.0 / (1.0 + jnp.exp(-logits)) - labels[...])
    grad = jnp.concatenate([grad[b : b + 1] for b in range(8)], axis=1)
    back = [grad * sums[w : w + 1, :] for w in range(8)] + [grad]

    def scatter(owner, masks):
        tall = jnp.concatenate([mask * value for value in back for mask in masks], axis=0)
        return dot(tall.astype(bf16), owner, 1, 1)

    own = scatter(owners[0], [rows[0:8, :]])
    listed = None
    for j in range(1, 5):
        owner = jnp.concatenate([owners[2 * j - 1], owners[2 * j]], axis=0)
        part = scatter(owner, [rows[16 * j - 8 + 8 * o : 16 * j + 8 * o, :] for o in range(2)])
        listed = part if listed is None else listed + part
    empty = jnp.zeros((8, LANES), f32)
    blocks = [[empty] * TILES for _ in range(16)]
    for w in range(9):
        for o in range(5):
            g, t = unit(w, o)
            at, side = 8 * (2 * w + (o - 1) % 2), LANES * ((o - 1) // 2)
            blocks[g][t] = listed[at : at + 8, side : side + LANES] if o else own[8 * w : 8 * w + 8]
    blocks = exchange(blocks)
    for z in range(send.shape[0]):
        send[z] = jnp.concatenate(blocks[z], axis=0).astype(bf16)


def total_kernel(came, send):
    lane = iota((8, LANES), 1)
    total = came[0].astype(f32)
    for z in range(1, came.shape[0]):
        total = total + came[z].astype(f32)
    tiles = split(total)
    values = [roll(tiles[q // SLOTS], q - 8 * (q % SLOTS)) for q in range(SLOTS * TILES)]
    for b in range(send.shape[0] // 4):
        at = (lane - b) & 31
        tile = jnp.zeros((8, LANES), f32)
        for q, value in enumerate(values):
            tile = jnp.where(at == q, value, tile)
        tile = roll(tile, -b).astype(bf16)
        for x in range(4):
            send[4 * b + x] = tile


def grad_kernel(users, came, enter_u, enter_i, leave_u, leave_i, bias_u, bias_i, head_u, head_i, out_u, out_i):
    lane = iota((8, LANES), 1)
    ranks = [jnp.zeros((8, LANES), f32)] * 10
    ats = [(lane - q) & 31 for q in range(10)]
    for p in range(came.shape[0]):
        tile = came[p].astype(f32)
        if p == 0:
            hits = [lane == (32 * o + 10 if o < 4 else 11) for o in range(5)]
            lines = [jnp.sum(jnp.where(hit, tile, 0.0), axis=1, keepdims=True) for hit in hits]
        tile = roll(tile, p)
        for q in range(10):
            ranks[q] = jnp.where(ats[q] == p, tile, ranks[q])
    ranks = [roll(v, -q) for q, v in enumerate(ranks)]
    low = jnp.concatenate(ranks[:5], axis=0)
    carry = jnp.concatenate(ranks[5:], axis=0)
    line = jnp.concatenate(lines, axis=0)
    held = low.shape[0]
    for out, a, b, enter, leave, bias, head in (
        (out_u, 0, users, enter_u, leave_u, bias_u, head_u),
        (out_i, users, held, enter_i, leave_i, bias_i, head_i),
    ):
        hidden = dot(low[a:b].astype(bf16), leave[...])
        back = dot(carry[a:b].astype(bf16), enter[...], 1, 1)
        out[...] = head[...] * (hidden + line[a:b] * (bias[...] + 1.0)) + back


def call(kernel, outs, flops, bytes_accessed, *args, fetch=False):
    many = isinstance(outs, list)
    spec = pl.BlockSpec(memory_space=pltpu.VMEM)
    if fetch:
        return pl.pallas_call(
            kernel,
            out_shape=outs,
            grid=(1,),
            in_specs=[pl.BlockSpec(a.shape, lambda i: (0, 0)) for a in args],
            out_specs=[spec] * len(outs) if many else spec,
            compiler_params=pltpu.CompilerParams(vmem_limit_bytes=60 * 1024 * 1024),
            cost_estimate=pl.CostEstimate(flops=flops, bytes_accessed=bytes_accessed, transcendentals=0),
        )(*args)
    return pl.pallas_call(
        kernel,
        out_shape=outs,
        in_specs=[spec] * len(args),
        out_specs=[spec] * len(outs) if many else spec,
        compiler_params=pltpu.CompilerParams(vmem_limit_bytes=40 * 1024 * 1024),
        cost_estimate=pl.CostEstimate(flops=flops, bytes_accessed=bytes_accessed, transcendentals=0),
    )(*args)


def swap(value, axes):
    return lax.all_to_all(value, axes, split_axis=0, concat_axis=0, tiled=True)


def body(
    user_table,
    user_scale,
    item_table,
    user_owner,
    user_row,
    item_owner,
    item_row,
    labels,
    enter_user,
    enter_item,
    leave_user,
    leave_item,
    bias_user,
    bias_item,
    head_user,
    head_item,
):
    depth = lax.axis_size("z")
    plane = lax.axis_size("y") * lax.axis_size("c") * lax.axis_size("x")
    users = user_table.shape[0]
    mass = labels.shape[0] * lax.axis_size("y") * lax.axis_size("c")
    block = 8 * TILES
    shape = jax.ShapeDtypeStruct
    weights = (enter_user, enter_item, leave_user, leave_item) + tuple(
        v[None] for v in (bias_user, bias_item, head_user, head_item)
    )

    send = call(
        parts_kernel, shape((plane, 8, LANES), bf16), 20_000_000, 2_500_000,
        user_table, user_scale[None], item_table, user_owner.T, user_row[None], item_owner.T, item_row.T, labels[None],
        *weights, fetch=True,
    )
    came = swap(send, BLOCK)
    send = call(share_kernel, shape((depth, block, LANES), bf16), 100_000, 200_000, came)
    table = swap(send, "z")
    owners, rows, targets = call(
        pick_kernel,
        [shape((9, LANES, mass), bf16), shape((72, mass), f32), shape((8, LANES), f32)],
        10_000_000, 3_000_000,
        came,
    )
    send, sums = call(
        fetch_kernel, [shape((plane, 8, LANES), bf16), shape((16, mass), f32)], 400_000_000, 3_000_000,
        table, owners, rows,
    )
    came = swap(send, BLOCK)
    send = call(
        back_kernel, shape((depth, block, LANES), bf16), 400_000_000, 3_000_000, came, targets, sums, owners, rows
    )
    came = swap(send, "z")
    send = call(total_kernel, shape((plane, 8, LANES), bf16), 100_000, 200_000, came)
    came = swap(send, BLOCK)
    user_grad, item_grad = call(
        lambda *refs: grad_kernel(users, *refs),
        [shape(user_table.shape, f32), shape(item_table.shape, f32)],
        20_000_000, 2_500_000,
        came, *weights,
    )
    return (user_grad, item_grad)


def solution(mesh):
    cols = mesh.shape["col"]
    cells = mesh.devices.reshape(-1, 16, 2, cols)
    fine = Mesh(cells, ("y", "z", "c", "x"))
    return jax.shard_map(
        body,
        mesh=fine,
        in_specs=(
            P(EMB, "x"),
            P(EMB),
            P(EMB, "x"),
            P(EMB, None),
            P(EMB),
            P(EMB, None),
            P(EMB, None),
            P(EMB),
            P("x", None),
            P("x", None),
            P(None, "x"),
            P(None, "x"),
            P("x"),
            P("x"),
            P("x"),
            P("x"),
        ),
        out_specs=(P(EMB, "x"), P(EMB, "x")),
        check_vma=False,
    )
```
